256 devices in a mesh: ctx: 64 (over z, y, core), tp: 4 (over x).
Axes of the slice: x: 4, y: 4, z: 8, core: 2. Of those that a mesh axis runs over, the one named last changes fastest.
Arguments:
- hidden: bfloat16 [8192, 5120], P('ctx'), may hold values from -12 to 12, as said below
- w_query: bfloat16 [5120, 2560], P('ctx', 'tp'), may hold values from -0.078125 to 0.078125
- w_keyval: bfloat16 [5120, 4, 256], P('ctx', 'tp'), may hold values from -0.078125 to 0.078125
- w_out: bfloat16 [2560, 5120], P('tp', 'ctx'), may hold values from -0.125 to 0.125
- episode_lengths: int32 [16], replicated, may hold values from 1 to 4096, 8192 in all
Outputs:
- attended: bfloat16 [8192, 5120], P('ctx', 'tp')
The draws below stay inside these ranges and needn't reach their ends.
Inputs may be any that keep to these rules, and one draw needn't show every extreme that they name: `hidden`: each row's entries are real numbers; no further structure is promised.
All inputs are finite; a program needn't handle non-finite values.
Results may differ from the reference program's by a relative error of at most 0.015.
The reference program's roundings to bfloat16 on the way (of `context`) count: a program that leaves them out, or rounds other values in their place, can miss the bound.
Values may be sent and summed in bfloat16 or wider, within the bound.
A program may use at most 64 MiB of HBM per device.

```python
import math
import jax
import jax.numpy as jnp
import numpy as np
from jax import lax

D = 5120
HQ = 20
HK = 4
HD = 128
NEP = 16
TOKENS = 8192
MOST_EP = 4096


def draw_hidden(key, part):
    key = jax.random.fold_in(key, 11)
    base_key = jax.random.fold_in(key, 0)
    values_out = jnp.clip(jax.random.normal(base_key, (TOKENS, D), jnp.float32), -5.0, 5.0)
    return values_out.astype(jnp.bfloat16)


def block_levels(key, shape, cuts, low, top_value):
    factor_of = 1.0
    for dim, blocks in cuts:
        heights = jax.random.uniform(jax.random.fold_in(jax.random.fold_in(key, 6), dim), (blocks,), jnp.float32, low / len(cuts), top_value / len(cuts))
        factor_of = factor_of * jnp.repeat(jnp.exp(heights), shape[dim] // blocks).reshape((-1,) + (1,) * (len(shape) - 1 - dim))
    return factor_of


def length_profile(count, total, limit, skew):
    weights = [(1 << 20) // math.isqrt(rank ** skew) + 1 for rank in range(2, count + 1)]
    surplus, holding = total - limit - (count - 1), [1] * (count - 1)
    while surplus > 0:
        candidates = [i for i in range(count - 1) if holding[i] < limit]
        pool, budget = sum([weights[i] for i in candidates]), surplus
        for i in candidates:
            extra = min(limit - holding[i], max(1, budget * weights[i] // pool), surplus)
            holding[i] = holding[i] + extra
            surplus = surplus - extra
    return np.array([limit] + holding)


def uneven_parts(key, number_of, total, limit, skew):
    if number_of == 2:
        one = jax.random.randint(key, (), max(1, total - limit), min(limit, total - 1) + 1)
        return jnp.stack([one, total - one])
    lengths = jnp.asarray(length_profile(number_of, total, limit, skew), jnp.int32)
    pairs = (number_of - 1) // 2
    giver, receiver = lengths[1:1 + 2 * pairs:2], lengths[2:2 + 2 * pairs:2]
    slack = jnp.minimum(giver - 1, limit - receiver)
    passed = jax.random.randint(jax.random.fold_in(key, 1), (pairs,), 0, 1 << 20) % (slack + 1)
    lengths = lengths.at[1:1 + 2 * pairs:2].set(giver - passed).at[2:2 + 2 * pairs:2].set(receiver + passed)
    return lengths[jax.random.permutation(jax.random.fold_in(key, 2), number_of)]


def centred(key, extent, deviation, reach, cuts=(), kind=jnp.bfloat16):
    entries = jax.random.normal(key, extent, jnp.float32) * deviation
    if len(cuts) > 0:
        entries = block_levels(key, extent, cuts, -0.22, 0.18) * entries
    return jnp.clip(entries, min=-reach, max=reach).astype(kind)


def setup_inputs(seed: int = 0) -> dict:
    key_of = jax.random.split(jax.random.key(seed), 6)
    hidden = draw_hidden(jax.random.fold_in(key_of[5], 71), 0)
    w_query = centred(key_of[1], (D, HQ * HD), D ** -0.5, 0.078125, ((0, 64), (1, 4)))
    w_keyval = centred(key_of[2], (D, HK, 2 * HD), D ** -0.5, 0.078125, ((0, 64), (1, 4)))
    w_out = centred(key_of[3], (HQ * HD, D), (HQ * HD) ** -0.5, 0.125, ((0, 4), (1, 64)))
    episode_lengths = uneven_parts(key_of[4], NEP, TOKENS, MOST_EP, 2).astype(jnp.int32)
    return dict(hidden=hidden, w_query=w_query, w_keyval=w_keyval, w_out=w_out, episode_lengths=episode_lengths)


def rotate(values_in, positions):
    half_dim = values_in.shape[-1] // 2
    freqs = 1000000.0 ** (-(jnp.arange(half_dim, dtype=jnp.float32) * 2.0) / values_in.shape[-1])
    angles = positions.astype(jnp.float32)[:, None] * freqs[None, :]
    cosine = jnp.cos(angles)[:, None, :]
    sine = jnp.sin(angles)[:, None, :]
    first_half = values_in[..., :half_dim]
    second_half = values_in[..., half_dim:]
    return jnp.concatenate([first_half * cosine - second_half * sine, second_half * cosine + first_half * sine], axis=-1)


def reference(hidden, w_query, w_keyval, w_out, episode_lengths):
    query = jnp.dot(hidden, w_query, preferred_element_type=jnp.float32).reshape(TOKENS, HQ, HD)
    keyval = jnp.dot(hidden, w_keyval.reshape(D, HK * 2 * HD), preferred_element_type=jnp.float32).reshape(TOKENS, HK, 2, HD)
    tokens_at = jnp.arange(TOKENS, dtype=jnp.int32)
    episode_ends = jnp.cumsum(episode_lengths).astype(jnp.int32)
    firsts = jnp.max(jnp.where(episode_ends[None, :] <= tokens_at[:, None], episode_ends[None, :], 0), axis=1).astype(jnp.int32)
    positions = tokens_at - firsts
    q_rot = rotate(query, positions).astype(jnp.bfloat16)
    k_rot = rotate(keyval[:, :, 0], positions).astype(jnp.bfloat16)
    v_all = keyval[:, :, 1].astype(jnp.bfloat16)
    group = HQ // HK
    q_block = min(512, TOKENS)
    window_len = min(TOKENS, MOST_EP + q_block)
    score_scale = 1.0 / (HD ** 0.5)

    def one_block(first_row):
        q_rows = lax.dynamic_slice_in_dim(q_rot, first_row, q_block, 0)
        key_first = jnp.clip(first_row + q_block - window_len, 0, TOKENS - window_len).astype(jnp.int32)
        k_rows = lax.dynamic_slice_in_dim(k_rot, key_first, window_len, 0)
        v_rows = lax.dynamic_slice_in_dim(v_all, key_first, window_len, 0)
        grouped = q_rows.reshape(q_block, HK, group, HD).astype(jnp.float32)
        scores = jnp.einsum('qhgd,khd->hgqk', grouped, k_rows.astype(jnp.float32)) * score_scale
        query_at = first_row + jnp.arange(q_block, dtype=jnp.int32)
        key_at = key_first + jnp.arange(window_len, dtype=jnp.int32)
        query_first = lax.dynamic_slice_in_dim(firsts, first_row, q_block, 0)
        allowed = (key_at[None, :] >= query_first[:, None]) & (key_at[None, :] <= query_at[:, None])
        scores = jnp.where(allowed, scores, -1e30)
        top = jnp.max(scores, axis=-1, keepdims=True)
        weights_exp = jnp.where(allowed, jnp.exp(scores - top), 0.0)
        totals = jnp.sum(weights_exp, axis=-1)
        rounded = lax.optimization_barrier(weights_exp.astype(jnp.bfloat16))
        mixed = jnp.einsum('hgqk,khd->hgqd', rounded.astype(jnp.float32), v_rows.astype(jnp.float32)) / totals[..., None]
        return jnp.transpose(mixed, (2, 0, 1, 3)).reshape(q_block, HQ * HD).astype(jnp.bfloat16)

    block_firsts = jnp.arange(TOKENS // q_block, dtype=jnp.int32) * q_block
    context = lax.map(one_block, block_firsts).reshape(TOKENS, HQ * HD)
    return jnp.dot(context, w_out, preferred_element_type=jnp.float32).astype(jnp.bfloat16)
```

```python
import functools
import math

import jax
import jax.numpy as jnp
import numpy as np
from jax import lax
from jax.experimental import pallas as pl
from jax.experimental.pallas import tpu as pltpu
from jax.sharding import PartitionSpec as P

MESH = pl.DeviceIdType.MESH
NZ, NY, NX = 8, 4, 4
ROWS = 128
HEADS = 5
HD = 128
NEG = -1e30
F32 = jnp.float32
BF = jnp.bfloat16


class Place:
    def __init__(self):
        index = lax.axis_index("ctx")
        self.index = index
        self.z = index // (2 * NY)
        self.y = lax.rem(index // 2, NY)
        self.c = lax.rem(index, 2)
        self.x = lax.axis_index("tp")

    def zof(self, dz):
        return lax.rem(self.z + (dz + NZ), NZ)

    def yof(self, dy):
        return lax.rem(self.y + (dy + NY), NY)

    def xof(self, dx):
        return lax.rem(self.x + (dx + NX), NX)

    def dev(self, dz=0, dy=0, dc=0, dx=0):
        c = 1 - self.c if dc else self.c
        return ((self.zof(dz) * NY + self.yof(dy)) * 2 + c, self.xof(dx))


def rcopy(src, dst, ssem, rsem, dev):
    return pltpu.make_async_remote_copy(
        src_ref=src, dst_ref=dst, send_sem=ssem, recv_sem=rsem, device_id=dev, device_id_type=MESH
    )


class Gather:
    def __init__(self, place, own, block, slab, sems, sign):
        self.p = place
        self.own = own
        self.block = block
        self.slab = slab
        self.zs, self.zr, self.ys, self.yr = sems
        self.sign = sign

    def zslot(self, r):
        if r <= 4:
            return self.p.zof(-self.sign * r)
        return self.p.zof(self.sign * (r - 4))

    def zcopy(self, core, hop, right):
        r = hop if right else (hop + 4 if hop else 0)
        z = self.zslot(r)
        dst = self.block(z, self.p.y) if core == 0 else self.slab(z)
        src = dst
        i = hop if right else 4 + hop
        j = hop + 1 if right else 5 + hop
        return rcopy(
            src, dst, self.zs.at[i], self.zr.at[j], self.p.dev(dz=self.sign if right else -self.sign)
        )

    def zwait(self, core, r):
        z = self.zslot(r)
        dst = self.block(z, self.p.y) if core == 0 else self.slab(z)
        rcopy(dst, dst, self.zs.at[0], self.zr.at[r], self.p.dev(dz=1)).wait_recv()

    def ycopy(self, r, k):
        ref = self.block(self.zslot(r), self.p.y)
        i = r * 3 + k - 1
        return rcopy(ref, ref, self.ys.at[i], self.yr.at[i], self.p.dev(dy=k))

    def ysend(self, r):
        for k in (1, 3, 2):
            self.ycopy(r, k).start()

    def ywait(self, r):
        for k in (1, 3, 2):
            i = r * 3 + k - 1
            ref = self.block(self.zslot(r), self.p.yof(-k))
            rcopy(ref, ref, self.ys.at[i], self.yr.at[i], self.p.dev(dy=k)).wait_recv()

    def start(self):
        @pl.when(self.p.c == 0)
        def _():
            self.zcopy(0, 0, True).start()
            self.zcopy(0, 0, False).start()

        self.ysend(0)

    def mid(self):
        self.ywait(0)

        @pl.when(self.p.c == 1)
        def _():
            self.zcopy(1, 0, True).start()
            self.zcopy(1, 0, False).start()

    def hop(self, s):
        for core in (0, 1):

            @pl.when(self.p.c == core)
            def _(core=core):
                self.zwait(core, s)
                if s < 4:
                    self.zcopy(core, s, True).start()
                    self.zwait(core, 4 + s)
                if s < 3:
                    self.zcopy(core, s, False).start()
                if core == 0:
                    self.ysend(s)
                    if s < 4:
                        self.ysend(4 + s)

    def ready(self, r):
        if r == 0:
            return

        @pl.when(self.p.c == 0)
        def _():
            self.ywait(r)

    def drain(self):
        for core in (0, 1):

            @pl.when(self.p.c == core)
            def _(core=core):
                for hop in range(4):
                    self.zcopy(core, hop, True).wait_send()
                for hop in range(3):
                    self.zcopy(core, hop, False).wait_send()
                for r in range(8) if core == 0 else (0,):
                    for k in (1, 2, 3):
                        self.ycopy(r, k).wait_send()


def kernel(
    lens, hid, wq, wkv, wot, freq, out,
    hh, wqb, wkvb, wob, kvb, acc_kv, acc_q, p_kv, p_q, qb, tok_first, cos_t, sin_t,
    m_s, l_s, a_s, ctx_t, xs, xr, x_own, f_send, f_recv, fin,
    *sems,
):
    p = Place()
    z, y, c, x = p.z, p.y, p.c, p.x
    a_sems, b_sems, d_sems = sems[0:4], sems[4:8], sems[8:12]
    c_zs, c_zr, c_ys, c_yr, c_ss, c_sr = sems[12:18]
    misc_s, misc_r, x_ss, x_sr = sems[18:22]

    barrier = pltpu.get_barrier_semaphore()
    peers = [dict(dz=1), dict(dz=-1), dict(dy=1), dict(dy=2), dict(dy=3), dict(dc=1), dict(dx=1), dict(dx=2), dict(dx=3)]
    for d in peers:
        pl.semaphore_signal(barrier, inc=1, device_id=p.dev(**d), device_id_type=MESH)

    wkvb[z, y, c] = wkv[...]
    wqb[z, y, c] = wq[...]
    wob[z, y] = wot[...]

    def clear(i, carry):
        wkvb[i // NY, lax.rem(i, NY), 1 - c] = jnp.zeros((80, 256), BF)
        wqb[i // NY, lax.rem(i, NY), 1 - c] = jnp.zeros((80, 640), BF)
        return carry

    lax.fori_loop(0, NZ * NY, clear, 0)
    hh[c] = hid[...]

    pl.semaphore_wait(barrier, len(peers))

    gather_a = Gather(
        p, wkv, lambda zz, yy: wkvb.at[zz, yy, c], lambda zz: wkvb.at[zz, :, c], a_sems, 1
    )
    gather_b = Gather(
        p, wq, lambda zz, yy: wqb.at[zz, yy, c], lambda zz: wqb.at[zz, :, c], b_sems, -1
    )
    gather_d = Gather(p, wot, lambda zz, yy: wob.at[zz, yy], lambda zz: wob.at[zz], d_sems, 1)

    def sibling(i, src, dst):
        return rcopy(src, dst, misc_s.at[i], misc_r.at[i], p.dev(dc=1))

    gather_a.start()
    hid_copy = sibling(0, hh.at[c], hh.at[c])
    hid_copy.start()
    gather_b.start()

    tok = p.index * ROWS + lax.broadcasted_iota(jnp.int32, (ROWS, HD), 0)
    first = jnp.zeros((ROWS, HD), jnp.int32)
    end = jnp.int32(0)
    for i in range(16):
        end = end + lens[i]
        first = jnp.maximum(first, jnp.where(end <= tok, end, 0))
    tok_first[...] = first
    angle = (tok - first).astype(F32) * freq[...]
    cos_t[...] = jnp.cos(angle)
    lane = lax.broadcasted_iota(jnp.int32, (ROWS, HD), 1)
    sine = jnp.sin(angle)
    sin_t[...] = jnp.where(lane < HD // 2, -sine, sine)

    def rotate(v):
        return v * cos_t[...] + pltpu.roll(v, HD // 2, 1) * sin_t[...]

    def project(gather, buf, acc, r, width, init=False):
        gather.ready(r)
        zz = gather.zslot(r)
        left = hh[:, :, pl.ds(pl.multiple_of(zz * 640, 128), 640)].reshape(2 * ROWS, 640)
        right = buf[zz].reshape(640, width)
        term = jnp.dot(left, right, preferred_element_type=F32).reshape(2, ROWS, width)
        if init:
            acc[...] = term
        else:
            acc[...] += term

    proj_a = functools.partial(project, gather_a, wkvb, acc_kv, width=256)
    proj_b = functools.partial(project, gather_b, wqb, acc_q, width=640)

    gather_a.mid()
    gather_a.hop(1)
    gather_b.mid()
    hid_copy.wait_recv()
    proj_a(r=0, init=True)
    gather_a.hop(2)
    proj_a(r=1)
    proj_a(r=5)
    gather_a.hop(3)
    proj_a(r=2)
    proj_a(r=6)
    gather_b.hop(1)
    gather_a.hop(4)
    proj_a(r=3)
    proj_a(r=7)
    proj_a(r=4)
    kv_copy = sibling(1, acc_kv.at[1 - c], p_kv)
    kv_copy.start()
    proj_b(r=0, init=True)
    kv_copy.wait_recv()
    keyval = acc_kv[c] + p_kv[...]
    kvb[z, c, y] = jnp.concatenate(
        [rotate(keyval[:, :HD]).astype(BF), keyval[:, HD:].astype(BF)], axis=1
    )

    def c_block(s, dy=0):
        return kvb.at[p.zof(-s), c, p.yof(dy)]

    def c_z(s):
        return rcopy(c_block(s), c_block(s), c_zs.at[s], c_zr.at[s + 1], p.dev(dz=1))

    def c_y(s, k):
        i = s * 3 + k - 1
        return rcopy(c_block(s), c_block(s), c_ys.at[i], c_yr.at[i], p.dev(dy=k))

    def c_sib(s):
        ref = kvb.at[p.zof(-s), c]
        return rcopy(ref, ref, c_ss.at[s], c_sr.at[s], p.dev(dc=1))

    def c_hop(s):
        if s:
            rcopy(c_block(s), c_block(s), c_zs.at[0], c_zr.at[s], p.dev(dz=1)).wait_recv()
        if s < 4:
            c_z(s).start()
        for k in (1, 3, 2):
            c_y(s, k).start()

    def c_plane(s):
        for k in (1, 3, 2):
            i = s * 3 + k - 1
            rcopy(c_block(s, -k), c_block(s, -k), c_ys.at[i], c_yr.at[i], p.dev(dy=k)).wait_recv()
        c_sib(s).start()

    def c_other(s):
        ref = kvb.at[p.zof(-s), 1 - c]
        rcopy(ref, ref, c_ss.at[s], c_sr.at[s], p.dev(dc=1)).wait_recv()

    c_hop(0)
    gather_b.hop(2)
    proj_b(r=1)
    proj_b(r=5)
    c_hop(1)
    c_plane(0)
    gather_b.hop(3)
    gather_d.start()
    proj_b(r=2)
    proj_b(r=6)
    c_hop(2)
    c_plane(1)
    gather_b.hop(4)
    proj_b(r=3)
    proj_b(r=7)
    c_hop(3)
    c_plane(2)
    gather_d.mid()
    proj_b(r=4)
    q_copy = sibling(2, acc_q.at[1 - c], p_q)
    q_copy.start()
    c_hop(4)
    c_plane(3)
    q_copy.wait_recv()
    query = acc_q[c] + p_q[...]
    for h in range(HEADS):
        qb[h] = rotate(query[:, h * HD : (h + 1) * HD]).astype(BF)
    gather_d.hop(1)

    scale = math.log2(math.e) / math.sqrt(HD)
    spot = lax.broadcasted_iota(jnp.int32, (ROWS, 4 * HD), 1)
    spot = (spot // ROWS) * (2 * ROWS) + lax.rem(spot, ROWS)
    wide_tok = p.index * ROWS + lax.broadcasted_iota(jnp.int32, (ROWS, 4 * HD), 0)

    def chunk(s, core, init=False):
        zp = p.zof(-s)
        key_at = spot + (zp * (2 * NY * ROWS) + core * ROWS)
        wide_first = jnp.concatenate([tok_first[...]] * 4, axis=1)
        bias = jnp.where((key_at >= wide_first) & (key_at <= wide_tok), 0.0, NEG)
        keys = kvb[zp, core, :, :, 0:HD].reshape(4 * ROWS, HD)
        values = kvb[zp, core, :, :, HD : 2 * HD].reshape(4 * ROWS, HD)
        for h in range(HEADS):
            score = lax.dot_general(
                qb[h], keys, (((1,), (1,)), ((), ())), preferred_element_type=F32
            )
            score = score * scale + bias
            top = jnp.broadcast_to(jnp.max(score, axis=1, keepdims=True), (ROWS, HD))
            if not init:
                old = m_s[h]
                top = jnp.maximum(old, top)
            weight = jnp.exp2(score - jnp.concatenate([top] * 4, axis=1))
            part = (weight[:, :HD] + weight[:, HD : 2 * HD]) + (
                weight[:, 2 * HD : 3 * HD] + weight[:, 3 * HD :]
            )
            mixed = jnp.dot(weight.astype(BF), values, preferred_element_type=F32)
            m_s[h] = top
            if init:
                l_s[h] = part
                a_s[h] = mixed
            else:
                factor = jnp.exp2(old - top)
                l_s[h] = l_s[h] * factor + part
                a_s[h] = a_s[h] * factor + mixed

    chunk(0, c, init=True)
    c_other(0)
    chunk(0, 1 - c)
    c_plane(4)
    for s in range(1, 5):
        if s < 4:
            gather_d.hop(s + 1)
        c_other(s)

        @pl.when(z >= s)
        def _(s=s):
            chunk(s, c)
            chunk(s, 1 - c)

    mine = pl.ds(pl.multiple_of(c * ROWS, ROWS), ROWS)
    for h in range(HEADS):
        total = jnp.sum(l_s[h], axis=1, keepdims=True)
        ctx_t[h * HD : (h + 1) * HD, mine] = jnp.transpose(a_s[h] / total).astype(BF)
    ctx_copy = sibling(3, ctx_t.at[:, mine], ctx_t.at[:, mine])
    ctx_copy.start()
    for r in range(8):
        gather_d.ready(r)
    ctx_copy.wait_recv()

    def x_copy(dx, half):
        i = (dx - 1) * 2 + half
        return rcopy(
            xs.at[dx - 1, half], xr.at[dx - 1, half], x_ss.at[i], x_sr.at[i], p.dev(dx=dx)
        )

    for dx in (2, 1, 3, 0):
        for half in (0, 1):
            zz = p.xof(dx) * 2 + half
            term = jnp.dot(
                wob[zz].reshape(320, 640), ctx_t[...], preferred_element_type=F32
            )
            if dx:
                xs[dx - 1, half] = term.astype(BF)
                x_copy(dx, half).start()
            else:
                x_own[half] = term
    for dx in (1, 3, 2):
        for half in (0, 1):
            x_copy(dx, half).wait_recv()
    for half in (0, 1):
        total = x_own[half] + (
            (xr[0, half].astype(F32) + xr[1, half].astype(F32)) + xr[2, half].astype(F32)
        )
        x_own[half] = total
    theirs = pl.ds(pl.multiple_of((1 - c) * ROWS, ROWS), ROWS)
    f_send[...] = x_own[:, :, theirs].astype(BF)
    fin_copy = sibling(4, f_send, f_recv)
    fin_copy.start()
    for half in (0, 1):
        fin[half, :, c] = x_own[half, :, mine].reshape(NY, 80, ROWS)
    fin_copy.wait_recv()
    for half in (0, 1):
        fin[half, :, 1 - c] = f_recv[half].astype(F32).reshape(NY, 80, ROWS)
    flat = fin[...].reshape(1280, ROWS)
    for i in range(10):
        out[:, i * ROWS : (i + 1) * ROWS] = jnp.transpose(
            flat[i * ROWS : (i + 1) * ROWS]
        ).astype(BF)

    gather_a.drain()
    gather_b.drain()
    gather_d.drain()
    for s in range(5):
        if s < 4:
            c_z(s).wait_send()
        for k in (1, 2, 3):
            c_y(s, k).wait_send()
        c_sib(s).wait_send()
    for cp in (hid_copy, kv_copy, q_copy, ctx_copy, fin_copy):
        cp.wait_send()
    for dx in (1, 2, 3):
        for half in (0, 1):
            x_copy(dx, half).wait_send()


def local(hidden, w_query, w_keyval, w_out, episode_lengths):
    half = np.arange(HD // 2, dtype=np.float64)
    freq = (1000000.0 ** (-(half * 2.0) / HD)).astype(np.float32)
    freq = jnp.asarray(np.concatenate([freq, freq])[None, :])
    vmem = pl.BlockSpec(memory_space=pltpu.VMEM)
    dma = pltpu.SemaphoreType.DMA
    gather_sems = [dma((7,)), dma((8,)), dma((24,)), dma((24,))]
    return pl.pallas_call(
        kernel,
        out_shape=jax.ShapeDtypeStruct((ROWS, 1280), BF),
        in_specs=[pl.BlockSpec(memory_space=pltpu.SMEM)] + [vmem] * 5,
        out_specs=vmem,
        scratch_shapes=[
            pltpu.VMEM((2, ROWS, 5120), BF),
            pltpu.VMEM((NZ, NY, 2, 80, 640), BF),
            pltpu.VMEM((NZ, NY, 2, 80, 256), BF),
            pltpu.VMEM((NZ, NY, 80, 640), BF),
            pltpu.VMEM((NZ, 2, NY, ROWS, 2 * HD), BF),
            pltpu.VMEM((2, ROWS, 256), F32),
            pltpu.VMEM((2, ROWS, 640), F32),
            pltpu.VMEM((ROWS, 256), F32),
            pltpu.VMEM((ROWS, 640), F32),
            pltpu.VMEM((HEADS, ROWS, HD), BF),
            pltpu.VMEM((ROWS, HD), jnp.int32),
            pltpu.VMEM((ROWS, HD), F32),
            pltpu.VMEM((ROWS, HD), F32),
            pltpu.VMEM((HEADS, ROWS, HD), F32),
            pltpu.VMEM((HEADS, ROWS, HD), F32),
            pltpu.VMEM((HEADS, ROWS, HD), F32),
            pltpu.VMEM((640, 2 * ROWS), BF),
            pltpu.VMEM((3, 2, 320, 2 * ROWS), BF),
            pltpu.VMEM((3, 2, 320, 2 * ROWS), BF),
            pltpu.VMEM((2, 320, 2 * ROWS), F32),
            pltpu.VMEM((2, 320, ROWS), BF),
            pltpu.VMEM((2, 320, ROWS), BF),
            pltpu.VMEM((2, NY, 2, 80, ROWS), F32),
        ]
        + gather_sems * 3
        + [dma((4,)), dma((5,)), dma((15,)), dma((15,)), dma((5,)), dma((5,))]
        + [dma((5,)), dma((5,)), dma((6,)), dma((6,))],
        name="layer",
        compiler_params=pltpu.CompilerParams(
            collective_id=0, has_side_effects=True, vmem_limit_bytes=56 * 2**20
        ),
    )(
        episode_lengths,
        hidden,
        w_query,
        w_keyval.reshape(80, 256),
        w_out.T,
        freq,
    )


def solution(mesh):
    placed = (P("ctx", None), P("ctx", "tp"), P("ctx", "tp", None), P("tp", "ctx"), P())
    return jax.shard_map(
        local, mesh=mesh, in_specs=placed, out_specs=P("ctx", "tp"), check_vma=False
    )
```

```python
import math

import jax
import jax.numpy as jnp
import numpy as np
from jax import lax
from jax.experimental import pallas as pl
from jax.experimental.pallas import tpu as pltpu
from jax.sharding import PartitionSpec as P

MESH = pl.DeviceIdType.MESH
NZ, NY, NX = 8, 4, 4
ROWS = 128
HEADS = 5
HD = 128
NEG = -1e30
F32 = jnp.float32
BF = jnp.bfloat16


class Place:
    def __init__(self):
        index = lax.axis_index("ctx")
        self.index = index
        self.z = index // (2 * NY)
        self.y = lax.rem(index // 2, NY)
        self.c = lax.rem(index, 2)
        self.x = lax.axis_index("tp")

    def zof(self, dz):
        return lax.rem(self.z + (dz + NZ), NZ)

    def yof(self, dy):
        return lax.rem(self.y + (dy + NY), NY)

    def xof(self, dx):
        return lax.rem(self.x + (dx + NX), NX)

    def dev(self, dz=0, dy=0, dc=0, dx=0):
        c = 1 - self.c if dc else self.c
        return ((self.zof(dz) * NY + self.yof(dy)) * 2 + c, self.xof(dx))


def rcopy(src, dst, ssem, rsem, dev):
    return pltpu.make_async_remote_copy(
        src_ref=src, dst_ref=dst, send_sem=ssem, recv_sem=rsem, device_id=dev, device_id_type=MESH
    )


class Ring:
    def __init__(self, place, block, sems, sign):
        self.p = place
        self.block = block
        self.zs, self.zr, self.ss, self.sr = sems
        self.sign = sign

    def zslot(self, r):
        if r <= 4:
            return self.p.zof(-self.sign * r)
        return self.p.zof(self.sign * (r - 4))

    def mine(self, r):
        return self.block(self.zslot(r), self.p.c)

    def zcopy(self, hop, right):
        ref = self.mine(hop if right or not hop else hop + 4)
        i, j = (hop, hop + 1) if right else (4 + hop, 5 + hop)
        step = self.sign if right else -self.sign
        return rcopy(ref, ref, self.zs.at[i], self.zr.at[j], self.p.dev(dz=step))

    def zwait(self, r):
        ref = self.mine(r)
        rcopy(ref, ref, self.zs.at[0], self.zr.at[r], self.p.dev(dz=1)).wait_recv()

    def pair(self, r):
        ref = self.mine(r)
        return rcopy(ref, ref, self.ss.at[r], self.sr.at[r], self.p.dev(dc=1))

    def ready(self, r):
        ref = self.block(self.zslot(r), 1 - self.p.c)
        rcopy(ref, ref, self.ss.at[r], self.sr.at[r], self.p.dev(dc=1)).wait_recv()

    def start(self):
        self.zcopy(0, True).start()
        self.zcopy(0, False).start()
        self.pair(0).start()

    def hop(self, s):
        self.zwait(s)
        if s < 4:
            self.zcopy(s, True).start()
            self.zwait(4 + s)
        if s < 3:
            self.zcopy(s, False).start()
        self.pair(s).start()
        if s < 4:
            self.pair(4 + s).start()

    def drain(self):
        for hop in range(4):
            self.zcopy(hop, True).wait_send()
        for hop in range(3):
            self.zcopy(hop, False).wait_send()
        for r in range(8):
            self.pair(r).wait_send()


class Tree(Ring):
    LEGS = ((0, 2, 2), (0, -2, 6), (0, 1, 1), (0, -1, 5), (2, 2, 4), (2, 1, 3), (6, -1, 7))

    def leg(self, i):
        slot, step, to = self.LEGS[i]
        ref = self.mine(slot)
        return rcopy(ref, ref, self.zs.at[i], self.zr.at[to], self.p.dev(dz=step))

    def start(self):
        for i in range(4):
            self.leg(i).start()
        self.pair(0).start()

    def arrive(self, slots, legs=()):
        for r in slots:
            self.zwait(r)
        for i in legs:
            self.leg(i).start()
        for r in slots:
            self.pair(r).start()

    def drain(self):
        for i in range(7):
            self.leg(i).wait_send()
        for r in range(8):
            self.pair(r).wait_send()


ORDER = (1, 3, 2)


def kernel(
    lens, hid, wq, wkv, wot, freq, out,
    hx, hr, wqb, wkvb, wob, kvb, acc_kv, acc_q, ks, kr, qs, qr, qb, tok_first, cos_t, sin_t,
    m_s, l_s, a_s, ctx_t, xs, xr, x_own,
    *sems,
):
    p = Place()
    z, y, c, x = p.z, p.y, p.c, p.x
    a_sems, b_sems, d_sems = sems[0:4], sems[4:8], sems[8:12]
    c_zs, c_zr, c_ys, c_yr, c_ss, c_sr = sems[12:18]
    h_ss, h_sr, g_ss, g_sr, k_ss, k_sr, q_ss, q_sr, d_ys, d_yr, x_ss, x_sr = sems[18:30]

    barrier = pltpu.get_barrier_semaphore()
    peers = [dict(dz=d) for d in (1, -1, 2, -2)]
    peers += [dict(dy=d) for d in (1, 2, 3)] + [dict(dc=1)] + [dict(dx=d) for d in (1, 2, 3)]
    for d in peers:
        pl.semaphore_signal(barrier, inc=1, device_id=p.dev(**d), device_id_type=MESH)

    wkvb[z, c] = wkv[...]
    wqb[z, c] = wq[...]
    wob[z, c, y] = wot[...]

    lane = lax.broadcasted_iota(jnp.int32, (ROWS, HD), 1)
    for yy in range(NY):
        shift = 32 * yy
        rest = [None, None]
        for zz in range(NZ):
            at = zz * 640 + 128 * yy
            w0 = hid[:, at : at + 128]
            w1 = hid[:, at + 128 : at + 256].astype(F32)
            if yy:
                back = HD - shift
                w0 = jnp.where(
                    lane < back,
                    pltpu.roll(w0.astype(F32), back, 1),
                    pltpu.roll(w1, back, 1),
                ).astype(BF)
            hx[yy, :, zz * 128 : (zz + 1) * 128] = w0
            turn = (32 * (zz % 4) - shift) % HD
            tail = pltpu.roll(w1, turn, 1) if turn else w1
            i = zz // 4
            rest[i] = tail if zz % 4 == 0 else jnp.where(lane // 32 == zz % 4, tail, rest[i])
        for i in range(2):
            hx[yy, :, 1024 + i * 128 : 1152 + i * 128] = rest[i].astype(BF)
    hr[y] = hx[y]

    for k in (1, 2, 3):

        @pl.when(y + k < NY)
        def _(k=k):
            kvb[z, c, y + k] = jnp.zeros((ROWS, 2 * HD), BF)

        @pl.when(y - k >= 0)
        def _(k=k):
            kvb[p.zof(-4), c, y - k] = jnp.zeros((ROWS, 2 * HD), BF)

    pl.semaphore_wait(barrier, len(peers))

    ring_a = Tree(p, lambda zz, cc: wkvb.at[zz, cc], a_sems, 1)
    ring_b = Ring(p, lambda zz, cc: wqb.at[zz, cc], b_sems, -1)
    ring_d = Ring(p, lambda zz, cc: wob.at[zz, cc], d_sems, 1)

    def part(xx):
        return pl.ds(pl.multiple_of(64 + 16 * xx, 16), 16)

    def h_copy(k):
        return rcopy(
            hx.at[p.yof(k), 0:64], hr.at[y, 0:64], h_ss.at[k - 1], h_sr.at[k - 1], p.dev(dy=k)
        )

    def h_part(k):
        return rcopy(
            hx.at[p.yof(k), part(x)], hr.at[y, part(x)], h_ss.at[k + 2], h_sr.at[k + 2],
            p.dev(dy=k),
        )

    def h_part_wait(k):
        ref = hr.at[p.yof(-k), part(x)]
        rcopy(ref, ref, h_ss.at[k + 2], h_sr.at[k + 2], p.dev(dy=k)).wait_recv()

    def h_on(k, dx, back=False):
        i = (k - 1) * 3 + dx - 1
        ref = hr.at[p.yof(-k), part(p.xof(-dx) if back else x)]
        return rcopy(ref, ref, g_ss.at[i], g_sr.at[i], p.dev(dx=dx))

    def k_copy(k):
        return rcopy(
            ks.at[p.yof(k)], kr.at[k - 1], k_ss.at[k - 1], k_sr.at[k - 1], p.dev(dy=k)
        )

    def q_copy(k):
        return rcopy(
            qs.at[p.yof(k)], qr.at[k - 1], q_ss.at[k - 1], q_sr.at[k - 1], p.dev(dy=k)
        )

    def d_copy(k, dy=0):
        ref = wob.at[z, c, p.yof(dy)]
        return rcopy(ref, ref, d_ys.at[k - 1], d_yr.at[k - 1], p.dev(dy=k))

    ring_a.start()
    for k in ORDER:
        h_part(k).start()
    for k in ORDER:
        h_copy(k).start()
    ring_b.start()

    tok = p.index * ROWS + lax.broadcasted_iota(jnp.int32, (ROWS, HD), 0)
    first = jnp.zeros((ROWS, HD), jnp.int32)
    end = jnp.int32(0)
    for i in range(16):
        end = end + lens[i]
        first = jnp.maximum(first, jnp.where(end <= tok, end, 0))
    tok_first[...] = first
    angle = (tok - first).astype(F32) * freq[...]
    cos_t[...] = jnp.cos(angle)
    sine = jnp.sin(angle)
    sin_t[...] = jnp.where(lane < HD // 2, -sine, sine)

    def rotate(v):
        return v * cos_t[...] + pltpu.roll(v, HD // 2, 1) * sin_t[...]

    def project(ring, buf, acc, send, r, width):
        if r < 8:
            ring.ready(r)
            zz = ring.zslot(r)
            left = hr[:, :, pl.ds(pl.multiple_of(zz * HD, HD), HD)].reshape(NY * ROWS, HD)
            right = buf[zz].reshape(160, width)[:HD]
        else:
            left = hr[:, :, 1024:1280].reshape(NY * ROWS, 256)
            right = buf[...].reshape(NZ, 160, width)[:, HD:].reshape(256, width)
        term = jnp.dot(left, right, preferred_element_type=F32).reshape(NY, ROWS, width)
        if r == 0:
            acc[...] = term
        elif r < 8:
            acc[...] += term
        else:
            term = acc[...] + term
            acc[...] = term
            send[...] = term.astype(BF)

    def c_block(s, dy=0):
        return kvb.at[p.zof(-s), c, p.yof(dy)]

    c_legs = ((0, 2, 2), (0, 1, 1), (0, -2, -2), (2, 1, 3), (-2, -2, 4))

    def c_z(i):
        plane, step, to = c_legs[i]
        return rcopy(
            c_block(plane), c_block(plane), c_zs.at[i], c_zr.at[max(to, 0)],
            p.dev(dz=step),
        )

    def c_zwait(s):
        ref = c_block(s)
        rcopy(ref, ref, c_zs.at[0], c_zr.at[max(s, 0)], p.dev(dz=1)).wait_recv()

    def c_y(s, k):
        i = s * 3 + k - 1
        return rcopy(c_block(s), c_block(s), c_ys.at[i], c_yr.at[i], p.dev(dy=k))

    def c_when(s, k, sending, act):
        if s == 0:
            pl.when(y + k < NY if sending else y - k >= 0)(act)
        elif s == 4:
            pl.when(y + k >= NY if sending else y - k < 0)(act)
        else:
            act()

    def c_sib(s):
        ref = kvb.at[p.zof(-s), c]
        return rcopy(ref, ref, c_ss.at[s], c_sr.at[s], p.dev(dc=1))

    def c_hop(s):
        if s:
            c_zwait(s)
        for i, leg in enumerate(c_legs):
            if leg[0] == s:
                c_z(i).start()
        if s < 0:
            return
        for k in ORDER:
            c_when(s, k, True, lambda: c_y(s, k).start())

    def c_plane(s):
        for k in ORDER:
            i = s * 3 + k - 1
            ref = c_block(s, -k)
            c_when(
                s, k, False,
                lambda: rcopy(ref, ref, c_ys.at[i], c_yr.at[i], p.dev(dy=k)).wait_recv(),
            )
        c_sib(s).start()

    def c_other(s):
        ref = kvb.at[p.zof(-s), 1 - c]
        rcopy(ref, ref, c_ss.at[s], c_sr.at[s], p.dev(dc=1)).wait_recv()

    ring_a.arrive((2, 6), (4, 5, 6))
    for k in ORDER:
        h_part_wait(k)
        for dx in ORDER:
            h_on(k, dx).start()
    ring_a.arrive((1, 5))
    ring_b.hop(1)
    ring_a.arrive((3, 4, 7))
    for k in ORDER:
        d_copy(k).start()
    ring_b.hop(2)
    for k in ORDER:
        h_copy(k).wait_recv()
        for dx in ORDER:
            h_on(k, dx, True).wait_recv()
    for r in (0, 1, 5, 2, 6, 3, 7, 4, 8):
        project(ring_a, wkvb, acc_kv, ks, r, 256)
    for k in ORDER:
        k_copy(k).start()
    ring_b.hop(3)
    for k in ORDER:
        d_copy(k, -k).wait_recv()
    ring_d.start()
    for k in ORDER:
        k_copy(k).wait_recv()
    keyval = (acc_kv[y] + kr[0].astype(F32)) + (kr[1].astype(F32) + kr[2].astype(F32))
    kvb[z, c, y] = jnp.concatenate(
        [rotate(keyval[:, :HD]).astype(BF), keyval[:, HD:].astype(BF)], axis=1
    )
    c_hop(0)
    ring_b.hop(4)
    for r in (0, 1, 5, 2, 6, 3, 7, 4, 8):
        project(ring_b, wqb, acc_q, qs, r, 640)
    for k in ORDER:
        q_copy(k).start()
    c_hop(2)
    c_hop(-2)
    c_hop(1)
    c_hop(3)
    c_hop(4)
    c_plane(0)
    c_plane(1)
    for k in ORDER:
        q_copy(k).wait_recv()
    query = (acc_q[y] + qr[0].astype(F32)) + (qr[1].astype(F32) + qr[2].astype(F32))
    for h in range(HEADS):
        qb[h] = rotate(query[:, h * HD : (h + 1) * HD]).astype(BF)
    ring_d.hop(1)
    c_plane(2)

    scale = math.log2(math.e) / math.sqrt(HD)
    spot = lax.broadcasted_iota(jnp.int32, (ROWS, 4 * HD), 1)
    spot = (spot // ROWS) * (2 * ROWS) + lax.rem(spot, ROWS)
    wide_tok = p.index * ROWS + lax.broadcasted_iota(jnp.int32, (ROWS, 4 * HD), 0)

    def chunk(s, core, init=False):
        zp = p.zof(-s)
        key_at = spot + (zp * (2 * NY * ROWS) + core * ROWS)
        wide_first = jnp.concatenate([tok_first[...]] * 4, axis=1)
        bias = jnp.where((key_at >= wide_first) & (key_at <= wide_tok), 0.0, NEG)
        keys = kvb[zp, core, :, :, 0:HD].reshape(4 * ROWS, HD)
        values = kvb[zp, core, :, :, HD : 2 * HD].reshape(4 * ROWS, HD)
        for h in range(HEADS):
            score = lax.dot_general(
                qb[h], keys, (((1,), (1,)), ((), ())), preferred_element_type=F32
            )
            score = score * scale + bias
            top = jnp.broadcast_to(jnp.max(score, axis=1, keepdims=True), (ROWS, HD))
            if not init:
                old = m_s[h]
                top = jnp.maximum(old, top)
            weight = jnp.exp2(score - jnp.concatenate([top] * 4, axis=1))
            part = (weight[:, :HD] + weight[:, HD : 2 * HD]) + (
                weight[:, 2 * HD : 3 * HD] + weight[:, 3 * HD :]
            )
            mixed = jnp.dot(weight.astype(BF), values, preferred_element_type=F32)
            m_s[h] = top
            if init:
                l_s[h] = part
                a_s[h] = mixed
            else:
                factor = jnp.exp2(old - top)
                l_s[h] = l_s[h] * factor + part
                a_s[h] = a_s[h] * factor + mixed

    chunk(0, c, init=True)
    c_other(0)
    chunk(0, 1 - c)
    c_plane(3)
    c_plane(4)
    for s in range(1, 5):
        c_other(s)

        @pl.when(z >= s)
        def _(s=s):
            chunk(s, c)
            chunk(s, 1 - c)

        if s == 2:
            ring_d.hop(2)

    for h in range(HEADS):
        total = jnp.sum(l_s[h], axis=1, keepdims=True)
        ctx_t[h * HD : (h + 1) * HD, :] = jnp.transpose(a_s[h] / total).astype(BF)

    def x_copy(dx, half):
        i = (dx - 1) * 2 + half
        return rcopy(
            xs.at[dx - 1, half], xr.at[dx - 1, half], x_ss.at[i], x_sr.at[i], p.dev(dx=dx)
        )

    for r in (0, 1, 5, 2, 6, 3, 7, 4):
        if r == 2:
            ring_d.hop(3)
        elif r == 3:
            ring_d.hop(4)
        ring_d.ready(r)
        zz = ring_d.zslot(r)
        half = lax.rem(zz, 2)
        dx = lax.rem(zz // 2 - x + NX, NX)
        term = jnp.dot(wob[zz].reshape(640, 640), ctx_t[...], preferred_element_type=F32)
        term = term.reshape(2, NY, 80, ROWS)

        @pl.when(dx == 0)
        def _(term=term, half=half):
            for core in (0, 1):
                x_own[half, :, core] = term[core]

        @pl.when(dx > 0)
        def _(term=term, half=half, dx=dx):
            for core in (0, 1):
                xs[dx - 1, half, :, core] = term[core].astype(BF)
            x_copy(dx, half).start()

    for half in (0, 1):
        for dx in ORDER:
            x_copy(dx, half).wait_recv()
        total = x_own[half] + (
            (xr[0, half].astype(F32) + xr[1, half].astype(F32)) + xr[2, half].astype(F32)
        )
        flat = total.reshape(640, ROWS)
        for i in range(5):
            out[:, half * 640 + i * ROWS : half * 640 + (i + 1) * ROWS] = jnp.transpose(
                flat[i * ROWS : (i + 1) * ROWS]
            ).astype(BF)

    ring_a.drain()
    ring_b.drain()
    ring_d.drain()
    for s in range(5):
        c_z(s).wait_send()
        for k in ORDER:
            c_when(s, k, True, lambda: c_y(s, k).wait_send())
        c_sib(s).wait_send()
    for k in ORDER:
        h_copy(k).wait_send()
        h_part(k).wait_send()
        for dx in ORDER:
            h_on(k, dx).wait_send()
        k_copy(k).wait_send()
        q_copy(k).wait_send()
        d_copy(k).wait_send()
        for half in (0, 1):
            x_copy(k, half).wait_send()


def local(hidden, w_query, w_keyval, w_out, episode_lengths):
    half = np.arange(HD // 2, dtype=np.float64)
    freq = (1000000.0 ** (-(half * 2.0) / HD)).astype(np.float32)
    freq = jnp.asarray(np.concatenate([freq, freq])[None, :])
    vmem = pl.BlockSpec(memory_space=pltpu.VMEM)
    dma = pltpu.SemaphoreType.DMA
    return pl.pallas_call(
        kernel,
        out_shape=jax.ShapeDtypeStruct((ROWS, 1280), BF),
        in_specs=[pl.BlockSpec(memory_space=pltpu.SMEM)] + [vmem] * 5,
        out_specs=vmem,
        scratch_shapes=[
            pltpu.VMEM((NY, ROWS, 1280), BF),
            pltpu.VMEM((NY, ROWS, 1280), BF),
            pltpu.VMEM((NZ, 2, 80, 640), BF),
            pltpu.VMEM((NZ, 2, 80, 256), BF),
            pltpu.VMEM((NZ, 2, NY, 80, 640), BF),
            pltpu.VMEM((NZ, 2, NY, ROWS, 2 * HD), BF),
            pltpu.VMEM((NY, ROWS, 256), F32),
            pltpu.VMEM((NY, ROWS, 640), F32),
            pltpu.VMEM((NY, ROWS, 256), BF),
            pltpu.VMEM((3, ROWS, 256), BF),
            pltpu.VMEM((NY, ROWS, 640), BF),
            pltpu.VMEM((3, ROWS, 640), BF),
            pltpu.VMEM((HEADS, ROWS, HD), BF),
            pltpu.VMEM((ROWS, HD), jnp.int32),
            pltpu.VMEM((ROWS, HD), F32),
            pltpu.VMEM((ROWS, HD), F32),
            pltpu.VMEM((HEADS, ROWS, HD), F32),
            pltpu.VMEM((HEADS, ROWS, HD), F32),
            pltpu.VMEM((HEADS, ROWS, HD), F32),
            pltpu.VMEM((640, ROWS), BF),
            pltpu.VMEM((3, 2, NY, 2, 80, ROWS), BF),
            pltpu.VMEM((3, 2, NY, 2, 80, ROWS), BF),
            pltpu.VMEM((2, NY, 2, 80, ROWS), F32),
        ]
        + [dma((7,)), dma((8,)), dma((8,)), dma((8,))] * 3
        + [dma((5,)), dma((5,)), dma((15,)), dma((15,)), dma((5,)), dma((5,))]
        + [dma((6,)), dma((6,)), dma((9,)), dma((9,))]
        + [dma((3,))] * 6
        + [dma((6,)), dma((6,))],
        name="layer",
        compiler_params=pltpu.CompilerParams(
            collective_id=0, has_side_effects=True, vmem_limit_bytes=56 * 2**20
        ),
    )(
        episode_lengths,
        hidden,
        w_query,
        w_keyval.reshape(80, 256),
        w_out.T,
        freq,
    )


def solution(mesh):
    placed = (P("ctx", None), P("ctx", "tp"), P("ctx", "tp", None), P("tp", "ctx"), P())
    return jax.shard_map(
        local, mesh=mesh, in_specs=placed, out_specs=P("ctx", "tp"), check_vma=False
    )
```

```python
import math

import jax
import jax.numpy as jnp
import numpy as np
from jax import lax
from jax.experimental import pallas as pl
from jax.experimental.pallas import tpu as pltpu
from jax.sharding import PartitionSpec as P

MESH = pl.DeviceIdType.MESH
NZ, NY, NX = 8, 4, 4
ROWS = 128
HEADS = 5
HD = 128
NEG = -1e30
F32 = jnp.float32
BF = jnp.bfloat16


class Place:
    def __init__(self):
        index = lax.axis_index("ctx")
        self.index = index
        self.z = index // (2 * NY)
        self.y = lax.rem(index // 2, NY)
        self.c = lax.rem(index, 2)
        self.x = lax.axis_index("tp")

    def zof(self, dz):
        return lax.rem(self.z + (dz + NZ), NZ)

    def yof(self, dy):
        return lax.rem(self.y + (dy + NY), NY)

    def xof(self, dx):
        return lax.rem(self.x + (dx + NX), NX)

    def dev(self, dz=0, dy=0, dc=0, dx=0):
        c = 1 - self.c if dc else self.c
        return ((self.zof(dz) * NY + self.yof(dy)) * 2 + c, self.xof(dx))


def rcopy(src, dst, ssem, rsem, dev):
    return pltpu.make_async_remote_copy(
        src_ref=src, dst_ref=dst, send_sem=ssem, recv_sem=rsem, device_id=dev, device_id_type=MESH
    )


class Ring:
    def __init__(self, place, block, sems, sign):
        self.p = place
        self.block = block
        self.zs, self.zr, self.ss, self.sr = sems
        self.sign = sign

    def zslot(self, r):
        if r <= 4:
            return self.p.zof(-self.sign * r)
        return self.p.zof(self.sign * (r - 4))

    def mine(self, r):
        return self.block(self.zslot(r), self.p.c)

    def zcopy(self, hop, right):
        ref = self.mine(hop if right or not hop else hop + 4)
        i, j = (hop, hop + 1) if right else (4 + hop, 5 + hop)
        step = self.sign if right else -self.sign
        return rcopy(ref, ref, self.zs.at[i], self.zr.at[j], self.p.dev(dz=step))

    def zwait(self, r):
        ref = self.mine(r)
        rcopy(ref, ref, self.zs.at[0], self.zr.at[r], self.p.dev(dz=1)).wait_recv()

    def pair(self, r):
        ref = self.mine(r)
        return rcopy(ref, ref, self.ss.at[r], self.sr.at[r], self.p.dev(dc=1))

    def ready(self, r):
        ref = self.block(self.zslot(r), 1 - self.p.c)
        rcopy(ref, ref, self.ss.at[r], self.sr.at[r], self.p.dev(dc=1)).wait_recv()

    def start(self):
        self.zcopy(0, True).start()
        self.zcopy(0, False).start()
        self.pair(0).start()

    def hop(self, s):
        self.zwait(s)
        if s < 4:
            self.zcopy(s, True).start()
            self.zwait(4 + s)
        if s < 3:
            self.zcopy(s, False).start()
        self.pair(s).start()
        if s < 4:
            self.pair(4 + s).start()

    def drain(self):
        for hop in range(4):
            self.zcopy(hop, True).wait_send()
        for hop in range(3):
            self.zcopy(hop, False).wait_send()
        for r in range(8):
            self.pair(r).wait_send()


class Tree(Ring):
    LEGS = ((0, 2, 2), (0, -2, 6), (0, 1, 1), (0, -1, 5), (2, 2, 4), (2, 1, 3), (6, -1, 7))

    def leg(self, i):
        slot, step, to = self.LEGS[i]
        ref = self.mine(slot)
        return rcopy(ref, ref, self.zs.at[i], self.zr.at[to], self.p.dev(dz=step))

    def start(self):
        for i in range(4):
            self.leg(i).start()
        self.pair(0).start()

    def arrive(self, slots, legs=()):
        for r in slots:
            self.zwait(r)
        for i in legs:
            self.leg(i).start()
        for r in slots:
            self.pair(r).start()

    def drain(self):
        for i in range(7):
            self.leg(i).wait_send()
        for r in range(8):
            self.pair(r).wait_send()


ORDER = (1, 3, 2)


def kernel(
    lens, hid, wq, wkv, wot, freq, out,
    hx, hr, wqb, wqc, wkvb, wob, kvb, acc_kv, acc_q, acc_r, ks, kr, qs, qr, rs, rr, qb, tok_first, cos_t, sin_t,
    m_s, l_s, a_s, ctx, xs, xr, x_own, f_send, f_recv, fin,
    *sems,
):
    p = Place()
    z, y, c, x = p.z, p.y, p.c, p.x
    a_sems, b_sems, e_sems, d_sems = sems[0:4], sems[4:8], sems[8:12], sems[12:16]
    c_zs, c_zr, c_ys, c_yr, c_ss, c_sr = sems[16:22]
    h_ss, h_sr, g_ss, g_sr, k_ss, k_sr, q_ss, q_sr, r_ss, r_sr, t_ss, t_sr, f_ss, f_sr, x_ss, x_sr = sems[22:38]

    barrier = pltpu.get_barrier_semaphore()
    peers = [dict(dz=d) for d in (1, -1, 2, -2)]
    peers += [dict(dy=d) for d in (1, 2, 3)] + [dict(dc=1)] + [dict(dx=d) for d in (1, 2, 3)]
    for d in peers:
        pl.semaphore_signal(barrier, inc=1, device_id=p.dev(**d), device_id_type=MESH)

    wkvb[z, c] = wkv[...]
    wqb[z, c] = wq[:, :256]
    wqc[z, c] = wq[:, 256:]
    wob[z, c] = wot[...]

    lane = lax.broadcasted_iota(jnp.int32, (ROWS, HD), 1)
    for yy in range(NY):
        shift = 32 * yy
        rest = [None, None]
        for zz in range(NZ):
            at = zz * 640 + 128 * yy
            w0 = hid[:, at : at + 128]
            w1 = hid[:, at + 128 : at + 256].astype(F32)
            if yy:
                back = HD - shift
                w0 = jnp.where(
                    lane < back,
                    pltpu.roll(w0.astype(F32), back, 1),
                    pltpu.roll(w1, back, 1),
                ).astype(BF)
            hx[yy, :, zz * 128 : (zz + 1) * 128] = w0
            turn = (32 * (zz % 4) - shift) % HD
            tail = pltpu.roll(w1, turn, 1) if turn else w1
            i = zz // 4
            rest[i] = tail if zz % 4 == 0 else jnp.where(lane // 32 == zz % 4, tail, rest[i])
        for i in range(2):
            hx[yy, :, 1024 + i * 128 : 1152 + i * 128] = rest[i].astype(BF)
    hr[y] = hx[y]

    for k in (1, 2, 3):

        @pl.when(y + k < NY)
        def _(k=k):
            kvb[z, c, y + k] = jnp.zeros((2, ROWS, HD), BF)

        @pl.when(y - k >= 0)
        def _(k=k):
            kvb[p.zof(-4), c, y - k] = jnp.zeros((2, ROWS, HD), BF)

    pl.semaphore_wait(barrier, len(peers))

    ring_a = Tree(p, lambda zz, cc: wkvb.at[zz, cc], a_sems, 1)
    ring_b = Ring(p, lambda zz, cc: wqb.at[zz, cc], b_sems, -1)
    ring_e = Ring(p, lambda zz, cc: wqc.at[zz, cc], e_sems, 1)
    ring_d = Ring(p, lambda zz, cc: wob.at[zz, cc], d_sems, -1)

    def part(xx):
        return pl.ds(pl.multiple_of(64 + 16 * xx, 16), 16)

    def h_copy(k):
        return rcopy(
            hx.at[p.yof(k), 0:64], hr.at[y, 0:64], h_ss.at[k - 1], h_sr.at[k - 1], p.dev(dy=k)
        )

    def h_part(k):
        return rcopy(
            hx.at[p.yof(k), part(x)], hr.at[y, part(x)], h_ss.at[k + 2], h_sr.at[k + 2],
            p.dev(dy=k),
        )

    def h_part_wait(k):
        ref = hr.at[p.yof(-k), part(x)]
        rcopy(ref, ref, h_ss.at[k + 2], h_sr.at[k + 2], p.dev(dy=k)).wait_recv()

    def h_on(k, dx, back=False):
        i = (k - 1) * 3 + dx - 1
        ref = hr.at[p.yof(-k), part(p.xof(-dx) if back else x)]
        return rcopy(ref, ref, g_ss.at[i], g_sr.at[i], p.dev(dx=dx))

    def k_copy(k):
        return rcopy(
            ks.at[p.yof(k)], kr.at[k - 1], k_ss.at[k - 1], k_sr.at[k - 1], p.dev(dy=k)
        )

    def q_copy(k):
        return rcopy(
            qs.at[p.yof(k)], qr.at[k - 1], q_ss.at[k - 1], q_sr.at[k - 1], p.dev(dy=k)
        )

    def r_copy(k):
        return rcopy(
            rs.at[p.yof(k)], rr.at[k - 1], r_ss.at[k - 1], r_sr.at[k - 1], p.dev(dy=k)
        )

    ring_a.start()
    for k in ORDER:
        h_part(k).start()
    for k in ORDER:
        h_copy(k).start()
    ring_b.start()

    tok = p.index * ROWS + lax.broadcasted_iota(jnp.int32, (ROWS, HD), 0)
    first = jnp.zeros((ROWS, HD), jnp.int32)
    end = jnp.int32(0)
    for i in range(16):
        end = end + lens[i]
        first = jnp.maximum(first, jnp.where(end <= tok, end, 0))
    row_tok = p.index * ROWS + lax.broadcasted_iota(jnp.int32, (1, ROWS), 1)
    row_first = jnp.zeros((1, ROWS), jnp.int32)
    end = jnp.int32(0)
    for i in range(16):
        end = end + lens[i]
        row_first = jnp.maximum(row_first, jnp.where(end <= row_tok, end, 0))
    tok_first[...] = row_first
    angle = (tok - first).astype(F32) * freq[...]
    cos_t[...] = jnp.cos(angle)
    sine = jnp.sin(angle)
    sin_t[...] = jnp.where(lane < HD // 2, -sine, sine)

    def rotate(v):
        return v * cos_t[...] + pltpu.roll(v, HD // 2, 1) * sin_t[...]

    def project(ring, buf, acc, send, r, width):
        if r < 8:
            ring.ready(r)
            zz = ring.zslot(r)
            left = hr[:, :, pl.ds(pl.multiple_of(zz * HD, HD), HD)].reshape(NY * ROWS, HD)
            right = buf[zz].reshape(160, width)[:HD]
        else:
            left = hr[:, :, 1024:1280].reshape(NY * ROWS, 256)
            right = buf[...].reshape(NZ, 160, width)[:, HD:].reshape(256, width)
        term = jnp.dot(left, right, preferred_element_type=F32).reshape(NY, ROWS, width)
        if r == 0:
            acc[...] = term
        elif r < 8:
            acc[...] += term
        else:
            term = acc[...] + term
            acc[...] = term
            send[...] = term.astype(BF)

    def c_block(s, dy=0):
        return kvb.at[p.zof(-s), c, p.yof(dy)]

    c_legs = ((0, 2, 2), (0, 1, 1), (0, -2, -2), (2, 1, 3), (-2, -2, 4))

    def c_z(i):
        plane, step, to = c_legs[i]
        return rcopy(
            c_block(plane), c_block(plane), c_zs.at[i], c_zr.at[max(to, 0)],
            p.dev(dz=step),
        )

    def c_zwait(s):
        ref = c_block(s)
        rcopy(ref, ref, c_zs.at[0], c_zr.at[max(s, 0)], p.dev(dz=1)).wait_recv()

    def c_y(s, k):
        i = s * 3 + k - 1
        return rcopy(c_block(s), c_block(s), c_ys.at[i], c_yr.at[i], p.dev(dy=k))

    def c_when(s, k, sending, act):
        if s == 0:
            pl.when(y + k < NY if sending else y - k >= 0)(act)
        elif s == 4:
            pl.when(y + k >= NY if sending else y - k < 0)(act)
        else:
            act()

    def c_sib(s):
        ref = kvb.at[p.zof(-s), c]
        return rcopy(ref, ref, c_ss.at[s], c_sr.at[s], p.dev(dc=1))

    def c_hop(s):
        if s:
            c_zwait(s)
        for i, leg in enumerate(c_legs):
            if leg[0] == s:
                c_z(i).start()
        if s < 0:
            return
        for k in ORDER:
            c_when(s, k, True, lambda: c_y(s, k).start())

    def c_plane(s):
        for k in ORDER:
            i = s * 3 + k - 1
            ref = c_block(s, -k)
            c_when(
                s, k, False,
                lambda: rcopy(ref, ref, c_ys.at[i], c_yr.at[i], p.dev(dy=k)).wait_recv(),
            )
        c_sib(s).start()

    def c_other(s):
        ref = kvb.at[p.zof(-s), 1 - c]
        rcopy(ref, ref, c_ss.at[s], c_sr.at[s], p.dev(dc=1)).wait_recv()

    ring_a.arrive((2, 6), (4, 5, 6))
    for k in ORDER:
        h_part_wait(k)
        for dx in ORDER:
            h_on(k, dx).start()
    ring_a.arrive((1, 5))
    ring_b.hop(1)
    ring_e.start()
    ring_a.arrive((3, 4, 7))
    ring_b.hop(2)
    for k in ORDER:
        h_copy(k).wait_recv()
        for dx in ORDER:
            h_on(k, dx, True).wait_recv()
    for r in (0, 1, 5, 2, 6, 3, 7, 4, 8):
        project(ring_a, wkvb, acc_kv, ks, r, 256)
    for k in ORDER:
        k_copy(k).start()
    ring_e.hop(1)
    ring_b.hop(3)
    for r in (0, 1, 5, 2, 6):
        project(ring_b, wqb, acc_q, qs, r, 256)
    ring_e.hop(2)
    ring_b.hop(4)
    for r in (3, 7, 4, 8):
        project(ring_b, wqb, acc_q, qs, r, 256)
    for k in ORDER:
        q_copy(k).start()
    ring_e.hop(3)
    for k in ORDER:
        k_copy(k).wait_recv()
    keyval = (acc_kv[y] + kr[0].astype(F32)) + (kr[1].astype(F32) + kr[2].astype(F32))
    kvb[z, c, y, 0] = rotate(keyval[:, :HD]).astype(BF)
    kvb[z, c, y, 1] = jnp.transpose(keyval[:, HD:]).astype(BF)
    c_hop(0)
    for r in (0, 1, 5, 2, 6):
        project(ring_e, wqc, acc_r, rs, r, 384)

    def queries(acc, got, copies, head, count):
        for k in ORDER:
            copies(k).wait_recv()
        query = (acc[y] + got[0].astype(F32)) + (got[1].astype(F32) + got[2].astype(F32))
        for h in range(count):
            qb[:, (head + h) * HD : (head + h + 1) * HD] = jnp.transpose(
                rotate(query[:, h * HD : (h + 1) * HD])
            ).astype(BF)

    queries(acc_q, qr, q_copy, 0, 2)

    scale = math.log2(math.e) / math.sqrt(HD)
    spot = lax.broadcasted_iota(jnp.int32, (NY * ROWS, ROWS), 0)
    spot = (spot // ROWS) * (2 * ROWS) + lax.rem(spot, ROWS)

    parts = (slice(0, 2 * ROWS), slice(2 * ROWS, HEADS * ROWS))

    def chunk(s, core, part, init=False):
        at = parts[part]
        zp = p.zof(-s)
        key_at = spot + (zp * (2 * NY * ROWS) + core * ROWS)
        bias = jnp.where((key_at >= tok_first[...]) & (key_at <= row_tok), 0.0, NEG)
        keys = kvb[zp, core, :, 0].reshape(NY * ROWS, HD)
        values = jnp.concatenate([kvb[zp, core, i, 1] for i in range(NY)], axis=1)
        score = jnp.dot(keys, qb[:, at], preferred_element_type=F32)
        score = score * scale + jnp.concatenate([bias] * (2 + part), axis=1)
        top = jnp.max(score, axis=0, keepdims=True)
        if not init:
            old = m_s[:, at]
            top = jnp.maximum(old, top)
        weight = jnp.exp2(score - top)
        share = jnp.sum(weight, axis=0, keepdims=True)
        mixed = jnp.dot(values, weight.astype(BF), preferred_element_type=F32)
        m_s[:, at] = top
        if init:
            l_s[:, at] = share
            a_s[:, at] = mixed
        else:
            factor = jnp.exp2(old - top)
            l_s[:, at] = l_s[:, at] * factor + share
            a_s[:, at] = a_s[:, at] * factor + mixed

    def reach(s, core, which=(0, 1)):
        @pl.when(z >= s)
        def _():
            for part in which:
                chunk(s, core, part)

    c_hop(2)
    c_hop(-2)
    ring_e.hop(4)
    for r in (3, 7, 4, 8):
        project(ring_e, wqc, acc_r, rs, r, 384)
    for k in ORDER:
        r_copy(k).start()
    c_hop(1)
    ring_d.start()
    c_plane(0)
    chunk(0, c, 0, init=True)
    ring_d.hop(1)
    c_hop(3)
    c_hop(4)
    c_other(0)
    chunk(0, 1 - c, 0)
    c_plane(1)
    c_plane(2)
    reach(1, c, (0,))
    queries(acc_r, rr, r_copy, 2, 3)
    chunk(0, c, 1, init=True)
    chunk(0, 1 - c, 1)
    ring_d.hop(2)
    reach(1, c, (1,))
    c_other(1)
    reach(1, 1 - c)
    c_plane(3)
    c_plane(4)
    reach(2, c)
    c_other(2)
    reach(2, 1 - c)
    ring_d.hop(3)
    reach(3, c)
    reach(4, c)
    c_other(3)
    reach(3, 1 - c)
    ring_d.hop(4)
    c_other(4)
    reach(4, 1 - c)

    for h in range(HEADS):
        at = slice(h * HD, (h + 1) * HD)
        ctx[y, at, :] = (a_s[:, at] / l_s[:, at]).astype(BF)

    def t_copy(k, dy=0):
        ref = ctx.at[p.yof(dy)]
        return rcopy(ref, ref, t_ss.at[k - 1], t_sr.at[k - 1], p.dev(dy=k))

    t_copy(1).start()
    t_copy(3).start()
    for r in range(8):
        ring_d.ready(r)

    def x_copy(g, dx):
        i = g * 3 + dx - 1
        return rcopy(
            xs.at[g, dx - 1], xr.at[g, dx - 1], x_ss.at[i], x_sr.at[i], p.dev(dx=dx)
        )

    def f_copy(g):
        return rcopy(
            f_send.at[g - 1], f_recv.at[g - 1], f_ss.at[g - 1], f_sr.at[g - 1], p.dev(dy=-g)
        )

    def settle(dy, part):
        part = part.reshape(2, 2, 80, ROWS)
        for half in (0, 1):
            fin[half, p.yof(dy)] = part[half]

    def terms(g):
        if g:
            t_copy(g, -g).wait_recv()
        for dx in (2, 1, 3, 0):
            right = ctx[p.yof(-g)]
            left = wob[pl.ds(2 * p.xof(dx), 2)].reshape(320, 640)
            term = jnp.dot(left, right, preferred_element_type=F32)
            if dx:
                xs[g, dx - 1] = term.astype(BF)
                x_copy(g, dx).start()
            else:
                x_own[g] = term

    def total(g):
        for dx in ORDER:
            x_copy(g, dx).wait_recv()
        part = x_own[g] + (
            (xr[g, 0].astype(F32) + xr[g, 1].astype(F32)) + xr[g, 2].astype(F32)
        )
        if g:
            f_send[g - 1] = part.astype(BF)
            f_copy(g).start()
        else:
            settle(0, part)

    terms(0)
    t_copy(2).start()
    for g in (1, 3, 2):
        terms(g)
    for g in (0, 1, 3, 2):
        total(g)
    for g in (1, 3, 2):
        f_copy(g).wait_recv()
        settle(g, f_recv[g - 1].astype(F32))
    flat = fin[...].reshape(1280, ROWS)
    for i in range(10):
        out[:, i * ROWS : (i + 1) * ROWS] = jnp.transpose(
            flat[i * ROWS : (i + 1) * ROWS]
        ).astype(BF)

    ring_a.drain()
    ring_b.drain()
    ring_e.drain()
    ring_d.drain()
    for s in range(5):
        c_z(s).wait_send()
        for k in ORDER:
            c_when(s, k, True, lambda: c_y(s, k).wait_send())
        c_sib(s).wait_send()
    for k in ORDER:
        h_copy(k).wait_send()
        h_part(k).wait_send()
        for dx in ORDER:
            h_on(k, dx).wait_send()
        k_copy(k).wait_send()
        q_copy(k).wait_send()
        r_copy(k).wait_send()
        t_copy(k).wait_send()
        f_copy(k).wait_send()
        for g in range(NY):
            x_copy(g, k).wait_send()


def local(hidden, w_query, w_keyval, w_out, episode_lengths):
    half = np.arange(HD // 2, dtype=np.float64)
    freq = (1000000.0 ** (-(half * 2.0) / HD)).astype(np.float32)
    freq = jnp.asarray(np.concatenate([freq, freq])[None, :])
    vmem = pl.BlockSpec(memory_space=pltpu.VMEM)
    dma = pltpu.SemaphoreType.DMA
    return pl.pallas_call(
        kernel,
        out_shape=jax.ShapeDtypeStruct((ROWS, 1280), BF),
        in_specs=[pl.BlockSpec(memory_space=pltpu.SMEM)] + [vmem] * 5,
        out_specs=vmem,
        scratch_shapes=[
            pltpu.VMEM((NY, ROWS, 1280), BF),
            pltpu.VMEM((NY, ROWS, 1280), BF),
            pltpu.VMEM((NZ, 2, 80, 256), BF),
            pltpu.VMEM((NZ, 2, 80, 384), BF),
            pltpu.VMEM((NZ, 2, 80, 256), BF),
            pltpu.VMEM((NZ, 2, 80, 640), BF),
            pltpu.VMEM((NZ, 2, NY, 2, ROWS, HD), BF),
            pltpu.VMEM((NY, ROWS, 256), F32),
            pltpu.VMEM((NY, ROWS, 256), F32),
            pltpu.VMEM((NY, ROWS, 384), F32),
            pltpu.VMEM((NY, ROWS, 256), BF),
            pltpu.VMEM((3, ROWS, 256), BF),
            pltpu.VMEM((NY, ROWS, 256), BF),
            pltpu.VMEM((3, ROWS, 256), BF),
            pltpu.VMEM((NY, ROWS, 384), BF),
            pltpu.VMEM((3, ROWS, 384), BF),
            pltpu.VMEM((HD, HEADS * ROWS), BF),
            pltpu.VMEM((1, ROWS), jnp.int32),
            pltpu.VMEM((ROWS, HD), F32),
            pltpu.VMEM((ROWS, HD), F32),
            pltpu.VMEM((1, HEADS * ROWS), F32),
            pltpu.VMEM((1, HEADS * ROWS), F32),
            pltpu.VMEM((HD, HEADS * ROWS), F32),
            pltpu.VMEM((NY, 640, ROWS), BF),
            pltpu.VMEM((NY, 3, 320, ROWS), BF),
            pltpu.VMEM((NY, 3, 320, ROWS), BF),
            pltpu.VMEM((NY, 320, ROWS), F32),
            pltpu.VMEM((3, 320, ROWS), BF),
            pltpu.VMEM((3, 320, ROWS), BF),
            pltpu.VMEM((2, NY, 2, 80, ROWS), F32),
        ]
        + [dma((7,)), dma((8,)), dma((8,)), dma((8,))] * 4
        + [dma((5,)), dma((5,)), dma((15,)), dma((15,)), dma((5,)), dma((5,))]
        + [dma((6,)), dma((6,)), dma((9,)), dma((9,))]
        + [dma((3,))] * 10
        + [dma((12,)), dma((12,))],
        name="layer",
        compiler_params=pltpu.CompilerParams(
            collective_id=0, has_side_effects=True, vmem_limit_bytes=56 * 2**20
        ),
    )(
        episode_lengths,
        hidden,
        w_query,
        w_keyval.reshape(80, 256),
        w_out.T,
        freq,
    )


def solution(mesh):
    placed = (P("ctx", None), P("ctx", "tp"), P("ctx", "tp", None), P("tp", "ctx"), P())
    return jax.shard_map(
        local, mesh=mesh, in_specs=placed, out_specs=P("ctx", "tp"), check_vma=False
    )
```

```python
import math

import jax
import jax.numpy as jnp
import numpy as np
from jax import lax
from jax.experimental import pallas as pl
from jax.experimental.pallas import tpu as pltpu
from jax.sharding import PartitionSpec as P

MESH = pl.DeviceIdType.MESH
NZ, NY, NX = 8, 4, 4
ROWS = 128
HEADS = 5
HD = 128
NEG = -1e30
F32 = jnp.float32
BF = jnp.bfloat16


class Place:
    def __init__(self):
        index = lax.axis_index("ctx")
        self.index = index
        self.z = index // (2 * NY)
        self.y = lax.rem(index // 2, NY)
        self.c = lax.rem(index, 2)
        self.x = lax.axis_index("tp")

    def zof(self, dz):
        return lax.rem(self.z + (dz + NZ), NZ)

    def yof(self, dy):
        return lax.rem(self.y + (dy + NY), NY)

    def xof(self, dx):
        return lax.rem(self.x + (dx + NX), NX)

    def dev(self, dz=0, dy=0, dc=0, dx=0):
        c = 1 - self.c if dc else self.c
        return ((self.zof(dz) * NY + self.yof(dy)) * 2 + c, self.xof(dx))


def rcopy(src, dst, ssem, rsem, dev):
    return pltpu.make_async_remote_copy(
        src_ref=src, dst_ref=dst, send_sem=ssem, recv_sem=rsem, device_id=dev, device_id_type=MESH
    )


class Ring:
    def __init__(self, place, block, sems, sign):
        self.p = place
        self.block = block
        self.zs, self.zr, self.ss, self.sr = sems
        self.sign = sign

    def zslot(self, r):
        if r <= 4:
            return self.p.zof(-self.sign * r)
        return self.p.zof(self.sign * (r - 4))

    def mine(self, r):
        return self.block(self.zslot(r), self.p.c)

    def zcopy(self, hop, right):
        ref = self.mine(hop if right or not hop else hop + 4)
        i, j = (hop, hop + 1) if right else (4 + hop, 5 + hop)
        step = self.sign if right else -self.sign
        return rcopy(ref, ref, self.zs.at[i], self.zr.at[j], self.p.dev(dz=step))

    def zwait(self, r):
        ref = self.mine(r)
        rcopy(ref, ref, self.zs.at[0], self.zr.at[r], self.p.dev(dz=1)).wait_recv()

    def pair(self, r):
        ref = self.mine(r)
        return rcopy(ref, ref, self.ss.at[r], self.sr.at[r], self.p.dev(dc=1))

    def ready(self, r):
        ref = self.block(self.zslot(r), 1 - self.p.c)
        rcopy(ref, ref, self.ss.at[r], self.sr.at[r], self.p.dev(dc=1)).wait_recv()

    def start(self):
        self.zcopy(0, True).start()
        self.zcopy(0, False).start()
        self.pair(0).start()

    def hop(self, s):
        self.zwait(s)
        if s < 4:
            self.zcopy(s, True).start()
            self.zwait(4 + s)
        if s < 3:
            self.zcopy(s, False).start()
        self.pair(s).start()
        if s < 4:
            self.pair(4 + s).start()

    def drain(self):
        for hop in range(4):
            self.zcopy(hop, True).wait_send()
        for hop in range(3):
            self.zcopy(hop, False).wait_send()
        for r in range(8):
            self.pair(r).wait_send()


class Tree(Ring):
    LEGS = ((0, 2, 2), (0, -2, 6), (0, 1, 1), (0, -1, 5), (2, 2, 4), (2, 1, 3), (6, -1, 7))

    def leg(self, i):
        slot, step, to = self.LEGS[i]
        ref = self.mine(slot)
        return rcopy(ref, ref, self.zs.at[i], self.zr.at[to], self.p.dev(dz=step))

    def start(self):
        for i in range(4):
            self.leg(i).start()
        self.pair(0).start()

    def arrive(self, slots, legs=()):
        for r in slots:
            self.zwait(r)
        for i in legs:
            self.leg(i).start()
        for r in slots:
            self.pair(r).start()

    def drain(self):
        for i in range(7):
            self.leg(i).wait_send()
        for r in range(8):
            self.pair(r).wait_send()


ORDER = (1, 3, 2)


def kernel(
    lens, hid, wq, wkv, wot, freq, out,
    hx, hr, wqb, wqc, wkvb, wob, kvb, acc_kv, acc_q, acc_r, ks, kr, qs, qr, rs, rr, qb, tok_first, cos_t, sin_t,
    m_s, l_s, a_s, ctx, xs, xr, x_own, f_send, f_recv, fin,
    *sems,
):
    p = Place()
    z, y, c, x = p.z, p.y, p.c, p.x
    a_sems, b_sems, e_sems, d_sems = sems[0:4], sems[4:8], sems[8:12], sems[12:16]
    c_zs, c_zr, c_ys, c_yr, c_ss, c_sr = sems[16:22]
    h_ss, h_sr, g_ss, g_sr, k_ss, k_sr, q_ss, q_sr, r_ss, r_sr, t_ss, t_sr, f_ss, f_sr, x_ss, x_sr = sems[22:38]

    barrier = pltpu.get_barrier_semaphore()
    peers = [dict(dz=d) for d in (1, -1, 2, -2)]
    peers += [dict(dy=d) for d in (1, 2, 3)] + [dict(dc=1)] + [dict(dx=d) for d in (1, 2, 3)]
    for d in peers:
        pl.semaphore_signal(barrier, inc=1, device_id=p.dev(**d), device_id_type=MESH)

    wkvb[z, c] = wkv[...]
    wqb[z, c] = wq[:, :256]
    wqc[z, c] = wq[:, 256:]
    wob[z, c] = wot[...]

    lane = lax.broadcasted_iota(jnp.int32, (ROWS, HD), 1)
    for yy in range(NY):
        shift = 32 * yy
        rest = [None, None]
        for zz in range(NZ):
            at = zz * 640 + 128 * yy
            w0 = hid[:, at : at + 128]
            w1 = hid[:, at + 128 : at + 256].astype(F32)
            if yy:
                back = HD - shift
                w0 = jnp.where(
                    lane < back,
                    pltpu.roll(w0.astype(F32), back, 1),
                    pltpu.roll(w1, back, 1),
                ).astype(BF)
            hx[yy, :, zz * 128 : (zz + 1) * 128] = w0
            turn = (32 * (zz % 4) - shift) % HD
            tail = pltpu.roll(w1, turn, 1) if turn else w1
            i = zz // 4
            rest[i] = tail if zz % 4 == 0 else jnp.where(lane // 32 == zz % 4, tail, rest[i])
        for i in range(2):
            hx[yy, :, 1024 + i * 128 : 1152 + i * 128] = rest[i].astype(BF)
    hr[y] = hx[y]

    for k in (1, 2, 3):

        @pl.when(y + k < NY)
        def _(k=k):
            kvb[z, c, y + k] = jnp.zeros((2, ROWS, HD), BF)

        @pl.when(y - k >= 0)
        def _(k=k):
            kvb[p.zof(-4), c, y - k] = jnp.zeros((2, ROWS, HD), BF)

    pl.semaphore_wait(barrier, len(peers))

    ring_a = Tree(p, lambda zz, cc: wkvb.at[zz, cc], a_sems, 1)
    ring_b = Ring(p, lambda zz, cc: wqb.at[zz, cc], b_sems, -1)
    ring_e = Ring(p, lambda zz, cc: wqc.at[zz, cc], e_sems, 1)
    ring_d = Ring(p, lambda zz, cc: wob.at[zz, cc], d_sems, -1)

    def part(xx):
        return pl.ds(pl.multiple_of(64 + 16 * xx, 16), 16)

    def h_copy(k):
        return rcopy(
            hx.at[p.yof(k), 0:64], hr.at[y, 0:64], h_ss.at[k - 1], h_sr.at[k - 1], p.dev(dy=k)
        )

    def h_part(k):
        return rcopy(
            hx.at[p.yof(k), part(x)], hr.at[y, part(x)], h_ss.at[k + 2], h_sr.at[k + 2],
            p.dev(dy=k),
        )

    def h_part_wait(k):
        ref = hr.at[p.yof(-k), part(x)]
        rcopy(ref, ref, h_ss.at[k + 2], h_sr.at[k + 2], p.dev(dy=k)).wait_recv()

    def h_on(k, dx, back=False):
        i = (k - 1) * 3 + dx - 1
        ref = hr.at[p.yof(-k), part(p.xof(-dx) if back else x)]
        return rcopy(ref, ref, g_ss.at[i], g_sr.at[i], p.dev(dx=dx))

    def k_copy(k):
        return rcopy(
            ks.at[p.yof(k)], kr.at[k - 1], k_ss.at[k - 1], k_sr.at[k - 1], p.dev(dy=k)
        )

    def q_copy(k):
        return rcopy(
            qs.at[p.yof(k)], qr.at[k - 1], q_ss.at[k - 1], q_sr.at[k - 1], p.dev(dy=k)
        )

    def r_copy(k):
        return rcopy(
            rs.at[p.yof(k)], rr.at[k - 1], r_ss.at[k - 1], r_sr.at[k - 1], p.dev(dy=k)
        )

    ring_a.start()
    for k in ORDER:
        h_part(k).start()
    for k in ORDER:
        h_copy(k).start()
    ring_b.start()

    tok = p.index * ROWS + lax.broadcasted_iota(jnp.int32, (ROWS, HD), 0)
    first = jnp.zeros((ROWS, HD), jnp.int32)
    end = jnp.int32(0)
    for i in range(16):
        end = end + lens[i]
        first = jnp.maximum(first, jnp.where(end <= tok, end, 0))
    row_tok = p.index * ROWS + lax.broadcasted_iota(jnp.int32, (1, ROWS), 1)
    row_first = jnp.zeros((1, ROWS), jnp.int32)
    end = jnp.int32(0)
    for i in range(16):
        end = end + lens[i]
        row_first = jnp.maximum(row_first, jnp.where(end <= row_tok, end, 0))
    tok_first[...] = row_first
    angle = (tok - first).astype(F32) * freq[...]
    cos_t[...] = jnp.cos(angle)
    sine = jnp.sin(angle)
    sin_t[...] = jnp.where(lane < HD // 2, -sine, sine)

    def rotate(v):
        return v * cos_t[...] + pltpu.roll(v, HD // 2, 1) * sin_t[...]

    def project(ring, buf, acc, send, r, width):
        if r < 8:
            ring.ready(r)
            zz = ring.zslot(r)
            left = hr[:, :, pl.ds(pl.multiple_of(zz * HD, HD), HD)].reshape(NY * ROWS, HD)
            right = buf[zz].reshape(160, width)[:HD]
        else:
            left = hr[:, :, 1024:1280].reshape(NY * ROWS, 256)
            right = buf[...].reshape(NZ, 160, width)[:, HD:].reshape(256, width)
        term = jnp.dot(left, right, preferred_element_type=F32).reshape(NY, ROWS, width)
        if r == 0:
            acc[...] = term
        elif r < 8:
            acc[...] += term
        else:
            term = acc[...] + term
            acc[...] = term
            send[...] = term.astype(BF)

    def c_block(s, dy=0):
        return kvb.at[p.zof(-s), c, p.yof(dy)]

    c_legs = ((0, 2, 2), (0, 1, 1), (0, -2, -2), (2, 1, 3), (-2, -2, 4))

    def c_z(i):
        plane, step, to = c_legs[i]
        return rcopy(
            c_block(plane), c_block(plane), c_zs.at[i], c_zr.at[max(to, 0)],
            p.dev(dz=step),
        )

    def c_zwait(s):
        ref = c_block(s)
        rcopy(ref, ref, c_zs.at[0], c_zr.at[max(s, 0)], p.dev(dz=1)).wait_recv()

    def c_y(s, k):
        i = s * 3 + k - 1
        return rcopy(c_block(s), c_block(s), c_ys.at[i], c_yr.at[i], p.dev(dy=k))

    def c_when(s, k, sending, act):
        if s == 0:
            pl.when(y + k < NY if sending else y - k >= 0)(act)
        elif s == 4:
            pl.when(y + k >= NY if sending else y - k < 0)(act)
        else:
            act()

    def c_sib(s):
        ref = kvb.at[p.zof(-s), c]
        return rcopy(ref, ref, c_ss.at[s], c_sr.at[s], p.dev(dc=1))

    def c_hop(s):
        if s:
            c_zwait(s)
        for i, leg in enumerate(c_legs):
            if leg[0] == s:
                c_z(i).start()
        if s < 0:
            return
        for k in ORDER:
            c_when(s, k, True, lambda: c_y(s, k).start())

    def c_plane(s):
        for k in ORDER:
            i = s * 3 + k - 1
            ref = c_block(s, -k)
            c_when(
                s, k, False,
                lambda: rcopy(ref, ref, c_ys.at[i], c_yr.at[i], p.dev(dy=k)).wait_recv(),
            )
        c_sib(s).start()

    def c_other(s):
        ref = kvb.at[p.zof(-s), 1 - c]
        rcopy(ref, ref, c_ss.at[s], c_sr.at[s], p.dev(dc=1)).wait_recv()

    ring_a.arrive((2, 6), (4, 5, 6))
    for k in ORDER:
        h_part_wait(k)
        for dx in ORDER:
            h_on(k, dx).start()
    ring_a.arrive((1, 5))
    ring_b.hop(1)
    ring_e.start()
    ring_a.arrive((3, 4, 7))
    ring_b.hop(2)
    for k in ORDER:
        h_copy(k).wait_recv()
        for dx in ORDER:
            h_on(k, dx, True).wait_recv()
    for r in (0, 1, 5, 2, 6, 3, 7, 4, 8):
        project(ring_a, wkvb, acc_kv, ks, r, 256)
    for k in ORDER:
        k_copy(k).start()
    ring_e.hop(1)
    ring_b.hop(3)
    for r in (0, 1, 5, 2, 6):
        project(ring_b, wqb, acc_q, qs, r, 256)
    ring_e.hop(2)
    ring_b.hop(4)
    for r in (3, 7, 4, 8):
        project(ring_b, wqb, acc_q, qs, r, 256)
    for k in ORDER:
        q_copy(k).start()
    ring_e.hop(3)
    for k in ORDER:
        k_copy(k).wait_recv()
    keyval = (acc_kv[y] + kr[0].astype(F32)) + (kr[1].astype(F32) + kr[2].astype(F32))
    kvb[z, c, y, 0] = rotate(keyval[:, :HD]).astype(BF)
    kvb[z, c, y, 1] = jnp.transpose(keyval[:, HD:]).astype(BF)
    c_hop(0)
    for r in (0, 1, 5, 2, 6):
        project(ring_e, wqc, acc_r, rs, r, 384)

    def queries(acc, got, copies, head, count):
        for k in ORDER:
            copies(k).wait_recv()
        query = (acc[y] + got[0].astype(F32)) + (got[1].astype(F32) + got[2].astype(F32))
        for h in range(count):
            qb[:, (head + h) * HD : (head + h + 1) * HD] = jnp.transpose(
                rotate(query[:, h * HD : (h + 1) * HD])
            ).astype(BF)

    queries(acc_q, qr, q_copy, 0, 2)

    scale = math.log2(math.e) / math.sqrt(HD)
    spot = lax.broadcasted_iota(jnp.int32, (NY * ROWS, ROWS), 0)
    spot = (spot // ROWS) * (2 * ROWS) + lax.rem(spot, ROWS)

    parts = (slice(0, 2 * ROWS), slice(2 * ROWS, HEADS * ROWS))

    def chunk(s, core, part, init=False):
        at = parts[part]
        zp = p.zof(-s)
        key_at = spot + (zp * (2 * NY * ROWS) + core * ROWS)
        bias = jnp.where((key_at >= tok_first[...]) & (key_at <= row_tok), 0.0, NEG)
        keys = kvb[zp, core, :, 0].reshape(NY * ROWS, HD)
        values = jnp.concatenate([kvb[zp, core, i, 1] for i in range(NY)], axis=1)
        score = jnp.dot(keys, qb[:, at], preferred_element_type=F32)
        score = score * scale + jnp.concatenate([bias] * (2 + part), axis=1)
        top = jnp.max(score, axis=0, keepdims=True)
        if not init:
            old = m_s[:, at]
            top = jnp.maximum(old, top)
        weight = jnp.exp2(score - top)
        share = jnp.sum(weight, axis=0, keepdims=True)
        mixed = jnp.dot(values, weight.astype(BF), preferred_element_type=F32)
        m_s[:, at] = top
        if init:
            l_s[:, at] = share
            a_s[:, at] = mixed
        else:
            factor = jnp.exp2(old - top)
            l_s[:, at] = l_s[:, at] * factor + share
            a_s[:, at] = a_s[:, at] * factor + mixed

    def reach(s, core, which=(0, 1)):
        @pl.when(z >= s)
        def _():
            for part in which:
                chunk(s, core, part)

    c_hop(2)
    c_hop(-2)
    c_hop(1)
    ring_e.hop(4)
    for r in (3, 7, 4, 8):
        project(ring_e, wqc, acc_r, rs, r, 384)
    for k in ORDER:
        r_copy(k).start()
    ring_d.start()
    c_plane(0)
    chunk(0, c, 0, init=True)
    c_hop(3)
    c_hop(4)
    ring_d.hop(1)
    c_other(0)
    chunk(0, 1 - c, 0)
    c_plane(1)
    c_plane(2)
    reach(1, c, (0,))
    ring_d.hop(2)
    queries(acc_r, rr, r_copy, 2, 3)
    chunk(0, c, 1, init=True)
    chunk(0, 1 - c, 1)
    reach(1, c, (1,))
    ring_d.hop(3)
    c_other(1)
    reach(1, 1 - c)
    c_plane(3)
    c_plane(4)
    reach(2, c)
    ring_d.hop(4)
    c_other(2)
    reach(2, 1 - c)
    reach(3, c)
    reach(4, c)
    c_other(3)
    reach(3, 1 - c)
    c_other(4)
    reach(4, 1 - c)

    for h in range(HEADS):
        at = slice(h * HD, (h + 1) * HD)
        ctx[y, at, :] = (a_s[:, at] / l_s[:, at]).astype(BF)

    def t_copy(k, dy=0):
        ref = ctx.at[p.yof(dy)]
        return rcopy(ref, ref, t_ss.at[k - 1], t_sr.at[k - 1], p.dev(dy=k))

    t_copy(1).start()
    t_copy(3).start()
    for r in range(8):
        ring_d.ready(r)

    def x_copy(g, dx):
        i = g * 3 + dx - 1
        return rcopy(
            xs.at[g, dx - 1], xr.at[g, dx - 1], x_ss.at[i], x_sr.at[i], p.dev(dx=dx)
        )

    def f_copy(g):
        return rcopy(
            f_send.at[g - 1], f_recv.at[g - 1], f_ss.at[g - 1], f_sr.at[g - 1], p.dev(dy=-g)
        )

    def settle(dy, part):
        part = part.reshape(2, 2, 80, ROWS)
        for half in (0, 1):
            fin[half, p.yof(dy)] = part[half]

    def terms(g):
        if g:
            t_copy(g, -g).wait_recv()
        for dx in (2, 1, 3, 0):
            right = ctx[p.yof(-g)]
            left = wob[pl.ds(2 * p.xof(dx), 2)].reshape(320, 640)
            term = jnp.dot(left, right, preferred_element_type=F32)
            if dx:
                xs[g, dx - 1] = term.astype(BF)
                x_copy(g, dx).start()
            else:
                x_own[g] = term

    def total(g):
        for dx in ORDER:
            x_copy(g, dx).wait_recv()
        part = x_own[g] + (
            (xr[g, 0].astype(F32) + xr[g, 1].astype(F32)) + xr[g, 2].astype(F32)
        )
        if g:
            f_send[g - 1] = part.astype(BF)
            f_copy(g).start()
        else:
            settle(0, part)

    terms(0)
    t_copy(2).start()
    for g in (1, 3, 2):
        terms(g)
    for g in (0, 1, 3, 2):
        total(g)
    for g in (1, 3, 2):
        f_copy(g).wait_recv()
        settle(g, f_recv[g - 1].astype(F32))
    flat = fin[...].reshape(1280, ROWS)
    for i in range(10):
        out[:, i * ROWS : (i + 1) * ROWS] = jnp.transpose(
            flat[i * ROWS : (i + 1) * ROWS]
        ).astype(BF)

    ring_a.drain()
    ring_b.drain()
    ring_e.drain()
    ring_d.drain()
    for s in range(5):
        c_z(s).wait_send()
        for k in ORDER:
            c_when(s, k, True, lambda: c_y(s, k).wait_send())
        c_sib(s).wait_send()
    for k in ORDER:
        h_copy(k).wait_send()
        h_part(k).wait_send()
        for dx in ORDER:
            h_on(k, dx).wait_send()
        k_copy(k).wait_send()
        q_copy(k).wait_send()
        r_copy(k).wait_send()
        t_copy(k).wait_send()
        f_copy(k).wait_send()
        for g in range(NY):
            x_copy(g, k).wait_send()


def local(hidden, w_query, w_keyval, w_out, episode_lengths):
    half = np.arange(HD // 2, dtype=np.float64)
    freq = (1000000.0 ** (-(half * 2.0) / HD)).astype(np.float32)
    freq = jnp.asarray(np.concatenate([freq, freq])[None, :])
    vmem = pl.BlockSpec(memory_space=pltpu.VMEM)
    dma = pltpu.SemaphoreType.DMA
    return pl.pallas_call(
        kernel,
        out_shape=jax.ShapeDtypeStruct((ROWS, 1280), BF),
        in_specs=[pl.BlockSpec(memory_space=pltpu.SMEM)] + [vmem] * 5,
        out_specs=vmem,
        scratch_shapes=[
            pltpu.VMEM((NY, ROWS, 1280), BF),
            pltpu.VMEM((NY, ROWS, 1280), BF),
            pltpu.VMEM((NZ, 2, 80, 256), BF),
            pltpu.VMEM((NZ, 2, 80, 384), BF),
            pltpu.VMEM((NZ, 2, 80, 256), BF),
            pltpu.VMEM((NZ, 2, 80, 640), BF),
            pltpu.VMEM((NZ, 2, NY, 2, ROWS, HD), BF),
            pltpu.VMEM((NY, ROWS, 256), F32),
            pltpu.VMEM((NY, ROWS, 256), F32),
            pltpu.VMEM((NY, ROWS, 384), F32),
            pltpu.VMEM((NY, ROWS, 256), BF),
            pltpu.VMEM((3, ROWS, 256), BF),
            pltpu.VMEM((NY, ROWS, 256), BF),
            pltpu.VMEM((3, ROWS, 256), BF),
            pltpu.VMEM((NY, ROWS, 384), BF),
            pltpu.VMEM((3, ROWS, 384), BF),
            pltpu.VMEM((HD, HEADS * ROWS), BF),
            pltpu.VMEM((1, ROWS), jnp.int32),
            pltpu.VMEM((ROWS, HD), F32),
            pltpu.VMEM((ROWS, HD), F32),
            pltpu.VMEM((1, HEADS * ROWS), F32),
            pltpu.VMEM((1, HEADS * ROWS), F32),
            pltpu.VMEM((HD, HEADS * ROWS), F32),
            pltpu.VMEM((NY, 640, ROWS), BF),
            pltpu.VMEM((NY, 3, 320, ROWS), BF),
            pltpu.VMEM((NY, 3, 320, ROWS), BF),
            pltpu.VMEM((NY, 320, ROWS), F32),
            pltpu.VMEM((3, 320, ROWS), BF),
            pltpu.VMEM((3, 320, ROWS), BF),
            pltpu.VMEM((2, NY, 2, 80, ROWS), F32),
        ]
        + [dma((7,)), dma((8,)), dma((8,)), dma((8,))] * 4
        + [dma((5,)), dma((5,)), dma((15,)), dma((15,)), dma((5,)), dma((5,))]
        + [dma((6,)), dma((6,)), dma((9,)), dma((9,))]
        + [dma((3,))] * 10
        + [dma((12,)), dma((12,))],
        name="layer",
        compiler_params=pltpu.CompilerParams(
            collective_id=0, has_side_effects=True, vmem_limit_bytes=56 * 2**20
        ),
    )(
        episode_lengths,
        hidden,
        w_query,
        w_keyval.reshape(80, 256),
        w_out.T,
        freq,
    )


def solution(mesh):
    placed = (P("ctx", None), P("ctx", "tp"), P("ctx", "tp", None), P("tp", "ctx"), P())
    return jax.shard_map(
        local, mesh=mesh, in_specs=placed, out_specs=P("ctx", "tp"), check_vma=False
    )
```
